32 devices in a mesh: rep: 2 (over y), grp: 4 (over x, core), loc: 4 (over z).
Axes of the slice: x: 2, y: 2, z: 4, core: 2. Of those that a mesh axis runs over, the one named last changes fastest.
Arguments:
- tokens: bfloat16 [256, 7168], P(('rep', 'grp', 'loc')), parts along dimension 0, may hold values from -6 to 6
- expert_ids: int32 [256, 8], P(('rep', 'grp', 'loc')), parts along dimension 0, may hold values from 0 to 15, as said below
- gate_values: bfloat16 [256, 8], P(('rep', 'grp', 'loc')), parts along dimension 0, may hold values from 0.049804688 to 0.59765625
- w_gate: bfloat16 [16, 7168, 1024], P(('grp', 'loc')), may hold values from -0.0625 to 0.0625
- w_up: bfloat16 [16, 7168, 1024], P(('grp', 'loc')), may hold values from -0.0625 to 0.0625
- w_down: bfloat16 [16, 1024, 7168], P(('grp', 'loc')), may hold values from -0.1875 to 0.1875
Outputs:
- mixed: bfloat16 [256, 7168], P(('rep', 'grp', 'loc')), parts along dimension 0
The draws below stay inside these ranges and needn't reach their ends.
There are 2 independent parts, one for each index of `rep`. The reference program is written for one: setup_inputs(seed, part) draws one part's arguments, and reference() takes and returns one part's arrays. A program takes and returns all parts, laid end to end along the dimension named above; an argument that names none is the same for every part. Nothing has to cross between parts.
Inputs may be any that keep to these rules, and one draw needn't show every extreme that they name: `expert_ids`: each row names 8 distinct experts, 2 in each of 4 distinct node groups, group g holding experts g * 4 to (g + 1) * 4 - 1. The rows of one device (aligned blocks of 8 rows) name any one expert at most 4 times. In every draw one group is named by every row, and each of its experts exactly 4 times by the rows of every device.
All inputs are finite; a program needn't handle non-finite values.
Results may differ from the reference program's by a relative error of at most 0.0065.
Values may be sent and summed in bfloat16 or wider, within the bound.
A program may use at most 128 MiB of HBM per device.

```python
import math
import jax
import jax.numpy as jnp
from jax import lax

D = 7168
FF = 1024
TOPK = 8
GSEL = 4
EXP_GROUP = 4
TOK_DEV = 8
PER_GROUP = 2
SPLIT = 1
FF_DEV = 1024
GROUPS = 4
EXPERTS = 16
TOKENS = 128
SLOTS = 64
N_GRP = 4
N_LOC = 4


def draw_expert_ids(key, part):
    key = jax.random.fold_in(key, 17)
    keys = jax.random.split(key, 4)
    blocks = N_GRP * N_LOC
    count = blocks * TOK_DEV
    columns = jnp.arange(N_GRP, dtype=jnp.int32)
    hottest = jax.random.randint(keys[0], (), 0, N_GRP)
    scores = jax.random.randint(keys[1], (count, N_GRP), 0, 1 << 20) * N_GRP + columns[None, :]
    scores = jnp.where(columns[None, :] == hottest, 1 << 30, scores)
    chosen = lax.top_k(scores, GSEL)[1].astype(jnp.int32)
    member = jnp.any(chosen[:, :, None] == columns[None, None, :], axis=1).astype(jnp.int32)
    member = member.reshape(blocks, TOK_DEV, N_GRP)
    ranked = (jnp.cumsum(member, axis=1) - member).reshape(count, N_GRP)
    rank_chosen = jnp.take_along_axis(ranked, chosen, axis=1)
    order_scores = jax.random.randint(keys[2], (blocks, N_GRP, EXP_GROUP), 0, 1 << 20) * EXP_GROUP + jnp.arange(EXP_GROUP, dtype=jnp.int32)
    sigma = jnp.argsort(order_scores, axis=-1).astype(jnp.int32)
    block_of = jnp.arange(count, dtype=jnp.int32) // TOK_DEV
    sigma_rows = sigma[block_of]
    sigma_chosen = jnp.take_along_axis(sigma_rows, chosen[:, :, None], axis=1)
    position = (PER_GROUP * rank_chosen[:, :, None] + jnp.arange(PER_GROUP, dtype=jnp.int32)[None, None, :]) % EXP_GROUP
    owners = jnp.take_along_axis(sigma_chosen, position, axis=2)
    named = (chosen[:, :, None] * EXP_GROUP + owners).reshape(count, TOPK)
    shuffle = jax.random.randint(keys[3], (count, TOPK), 0, 1 << 20) * TOPK + jnp.arange(TOPK, dtype=jnp.int32)
    placing = jnp.argsort(shuffle, axis=1)
    return jnp.take_along_axis(named, placing, axis=1).astype(jnp.int32)


def steps_of(stream_key, dims, cuts, least, largest):
    factor_of = 1.0
    for dim, blocks in cuts:
        steps = jax.random.uniform(jax.random.fold_in(jax.random.fold_in(stream_key, 6), dim), (blocks,), jnp.float32, least / len(cuts), largest / len(cuts))
        factor_of = factor_of * jnp.repeat(jnp.exp(steps), dims[dim] // blocks).reshape((-1,) + (1,) * (len(dims) - 1 - dim))
    return factor_of


def noise(own_key, shape, spread, bound, cuts=(), kind=jnp.bfloat16):
    gain = steps_of(own_key, shape, cuts, -0.22, 0.18) if cuts else 1.0
    result = jax.random.normal(own_key, shape, jnp.float32) * spread * gain
    return jnp.minimum(jnp.maximum(result, -bound), bound).astype(kind)


def setup_inputs(seed: int = 0, part: int = 0) -> dict:
    seeds = jax.random.split(jax.random.key(seed), 7)
    part_keys = jax.random.split(jax.random.fold_in(seeds[6], part), 7)
    tokens = noise(part_keys[0], (TOKENS, D), 1.0, 6.0, ((0, 16),))
    expert_ids = draw_expert_ids(jax.random.fold_in(jax.random.fold_in(seeds[6], part), 71), part)
    gate_values = jnp.clip(jnp.exp(math.log(0.59765625) - 2.4849066 * jax.random.uniform(part_keys[2], (TOKENS, TOPK), jnp.float32) ** steps_of(part_keys[2], (TOKENS, TOPK), ((0, 16),), -0.2, 0.2)), 0.049804688, 0.59765625).astype(jnp.bfloat16)
    w_gate = noise(seeds[3], (EXPERTS * SPLIT, D, FF_DEV), D ** -0.5, 0.0625, ((0, 16),))
    w_up = noise(seeds[4], (EXPERTS * SPLIT, D, FF_DEV), D ** -0.5, 0.0625, ((0, 16),))
    w_down = noise(seeds[5], (EXPERTS * SPLIT, FF_DEV, D), FF ** -0.5, 0.1875, ((0, 16),))
    return dict(tokens=tokens, expert_ids=expert_ids, gate_values=gate_values, w_gate=w_gate, w_up=w_up, w_down=w_down)


def reference(tokens, expert_ids, gate_values, w_gate, w_up, w_down):
    flat_ids = expert_ids.reshape(-1).astype(jnp.int32)
    flat_gate = gate_values.reshape(-1).astype(jnp.float32)
    count = flat_ids.shape[0]

    def one_block(block):
        expert = (block // SPLIT).astype(jnp.int32)
        picked = jnp.nonzero(flat_ids == expert, size=SLOTS, fill_value=count)[0].astype(jnp.int32)
        valid = picked < count
        safe = jnp.minimum(picked, count - 1)
        row_index = (safe // TOPK).astype(jnp.int32)
        rows = tokens[row_index]
        gate_part = jnp.dot(rows, w_gate[block], preferred_element_type=jnp.float32)
        up_part = jnp.dot(rows, w_up[block], preferred_element_type=jnp.float32)
        hidden = (jax.nn.silu(gate_part) * up_part).astype(jnp.bfloat16)
        down = jnp.dot(hidden, w_down[block], preferred_element_type=jnp.float32)
        weight = jnp.where(valid, flat_gate[safe], jnp.zeros_like(flat_gate[safe]))
        item = (down * weight[:, None]).astype(jnp.bfloat16)
        return item, row_index

    def one_group(total, group):
        blocks = (group * EXP_GROUP * SPLIT + jnp.arange(EXP_GROUP * SPLIT, dtype=jnp.int32)).astype(jnp.int32)
        items, row_index = lax.map(one_block, blocks)
        items = lax.optimization_barrier(items)
        partial_value = jnp.zeros((TOKENS, D), jnp.float32).at[row_index.reshape(-1)].add(items.reshape(-1, D).astype(jnp.float32))
        rounded = lax.optimization_barrier(partial_value.astype(jnp.bfloat16))
        return total + rounded.astype(jnp.float32), None

    total, unused = lax.scan(one_group, jnp.zeros((TOKENS, D), jnp.float32), jnp.arange(GROUPS, dtype=jnp.int32))
    return total.astype(jnp.bfloat16)
```

```python
import functools

import jax
import jax.numpy as jnp
from jax import lax
from jax.experimental import pallas as pl
from jax.experimental.pallas import tpu as pltpu
from jax.sharding import PartitionSpec as P

EXP_GROUP = 4
LANES = 128
C_IN = 2
C_OUT = 4
F32 = jnp.float32
BF16 = jnp.bfloat16


def al(v, m):
    return pl.multiple_of(v, m)


def kernel(nx, nz, tok_ref, ids_ref, gv_ref, wg_hbm, wu_hbm, wd_hbm, out_ref,
           wg, wu, wd, pk, pk_in, gat, gts, acc_g, acc_u, hid, snd, tin, xin, zl, zr, zsl, zsr, res, fin, fin_in,
           w_sem, wd_sem, pk_sem, gts_s, gts_r, zs, zv, xs, xv, cs, cv, ss, sr, xos, xor, zos, zor, fs, fr):
    rows, width = tok_ref.shape
    half = width // 2
    blk = 2 * rows
    nb = nx * nz
    total = nb * blk
    wi = half // C_IN
    wo = half // C_OUT
    ff = wg.shape[1]
    g = lax.axis_index("grp")
    z = lax.axis_index("loc")
    x = g // 2
    c = g % 2
    other = 1 - c
    mate = x * 2 + other

    def rc(src, dst, s, r, grp=None, loc=None):
        return pltpu.make_async_remote_copy(
            src_ref=src, dst_ref=dst, send_sem=s, recv_sem=r,
            device_id={"grp": g if grp is None else grp, "loc": z if loc is None else loc},
            device_id_type=pl.DeviceIdType.MESH)

    def w_copy(i, k):
        src, dst = ((wg_hbm, wg), (wu_hbm, wu))[i]
        return pltpu.make_async_copy(src.at[0, pl.ds(k * wi, wi), :], dst.at[pl.ds(k * wi, wi), :], w_sem.at[i, k])

    def wd_copy(h, j):
        return pltpu.make_async_copy(
            wd_hbm.at[0, :, pl.ds(al(h * half + j * wo, LANES), wo)], wd.at[h * C_OUT + j], wd_sem.at[h * C_OUT + j])

    for j in range(C_IN):
        for h in range(2):
            for i in range(2):
                w_copy(i, h * C_IN + j).start()
    for j in range(C_OUT):
        wd_copy(other, j).start()
        wd_copy(c, j).start()

    barrier = pltpu.get_barrier_semaphore()

    def chips():
        for dx in range(nx):
            for dz in range(nz):
                if dx or dz:
                    yield dx * nz + dz - 1, lax.rem(x + dx, nx), lax.rem(z + dz, nz)

    pl.semaphore_signal(barrier, inc=1, device_id={"grp": mate, "loc": z}, device_id_type=pl.DeviceIdType.MESH)
    for _, xb, zb in chips():
        pl.semaphore_signal(barrier, inc=1, device_id={"grp": xb * 2 + c, "loc": zb},
                            device_id_type=pl.DeviceIdType.MESH)

    tok = tok_ref[...].astype(F32)
    lane = lax.broadcasted_iota(jnp.int32, (rows, LANES), 1)
    ids = ids_ref[...]
    gv = gv_ref[...].astype(F32)
    dense = jnp.zeros((rows, LANES), F32)
    for k in range(ids.shape[1]):
        dense = dense + jnp.where(lane == ids[:, k:k + 1], gv[:, k:k + 1], 0.0)
    pk[:, :half] = jnp.concatenate([tok[:, :half], tok[:, half:]], axis=0).astype(BF16)
    pk[:, half:] = jnp.concatenate([dense, dense], axis=0).astype(BF16)
    pl.semaphore_wait(barrier, nb)
    swap = rc(pk, pk_in, pk_sem.at[0], pk_sem.at[1], grp=mate)
    swap.start()

    def rows_of(xb, zb):
        return pl.ds(al((xb * nz + zb) * blk, blk), blk)

    swap.wait_recv()
    mine, theirs = pk[...].astype(F32), pk_in[...].astype(F32)
    a = jnp.where(c == 0, mine, theirs)
    b = jnp.where(c == 0, theirs, mine)
    for h in range(2):
        both = jnp.concatenate([a[h * rows:(h + 1) * rows, :half], b[h * rows:(h + 1) * rows, :half]], axis=0)
        both = both.astype(BF16)
        for j in range(C_IN):
            gat[h * C_IN + j, rows_of(x, z), :] = both[:, j * wi:(j + 1) * wi]
    gts[rows_of(x, z), :] = jnp.concatenate([a[:rows, half:], b[:rows, half:]], axis=0).astype(BF16)

    sends = []

    def go(cond, cp):
        sends.append((cond, cp))
        if cond is None:
            cp.start()
        else:
            pl.when(cond)(cp.start)

    def both_conds(p, q):
        return p if q is None else q if p is None else jnp.logical_and(p, q)

    def piece(h, j, xb, zb):
        return gat.at[h * C_IN + j, rows_of(xb, zb), :]

    def zcopy(way, j, d, zb):
        p = piece(c, j, x, zb)
        return rc(p, p, zs.at[way, j, d], zv.at[way, j, d], loc=z + 1 if way == 0 else z - 1)

    def xcopy(j, xd, slot, xb, zb, to):
        p = piece(c, j, xb, zb)
        return rc(p, p, xs.at[j, xd - 1, slot], xv.at[j, xd - 1, slot], grp=to * 2 + c)

    def ccopy(h, j, xd, slot, xb, zb):
        p = piece(h, j, xb, zb)
        return rc(p, p, cs.at[j, xd, slot], cv.at[j, xd, slot], grp=mate)

    can = (z + 1 < nz, z >= 1)

    def spread(cond, j, slot, zb):
        for xd in range(1, nx):
            go(cond, xcopy(j, xd, slot, x, zb, lax.rem(x + xd, nx)))

    for j in range(C_IN):
        for way in range(2):
            go(can[way], zcopy(way, j, 0, z))
        spread(None, j, 0, z)
    for n, xb, zb in chips():
        p = gts.at[rows_of(x, z), :]
        go(None, rc(p, p, gts_s.at[n], gts_r.at[n], grp=xb * 2 + c, loc=zb))

    def slots(d):
        if d == 0:
            return [(None, 0, z)]
        return [(z >= d, d, z - d), (z + d < nz, nz - 1 + d, z + d)]

    def x_arrivals(d, j):
        for cond, slot, zb in slots(d):
            for xd in range(1, nx):
                xb = lax.rem(x + nx - xd, nx)

                def take():
                    xcopy(j, xd, slot, xb, zb, x).wait_recv()
                    ccopy(c, j, xd, slot, xb, zb).start()
                if cond is None:
                    take()
                else:
                    pl.when(cond)(take)
                sends.append((cond, ccopy(c, j, xd, slot, xb, zb)))

    for d in range(1, nz):
        for j in range(C_IN):
            for way, (cond, slot, zb) in enumerate(slots(d)):
                pl.when(cond)(zcopy(way, j, d - 1, zb).wait_recv)
                if d < nz - 1:
                    go(both_conds(cond, can[way]), zcopy(way, j, d, zb))
                spread(cond, j, slot, zb)
                go(cond, ccopy(c, j, 0, slot, x, zb))
            x_arrivals(d - 1, j)
    for j in range(C_IN):
        x_arrivals(nz - 1, j)

    mt = min(LANES, total)
    nt = min(256, ff)
    for j in range(C_IN):
        for d in range(nz):
            for cond, slot, zb in slots(d):
                for xd in range(0 if d else 1, nx):
                    cp = ccopy(other, j, xd, slot, lax.rem(x + nx - xd, nx), zb)
                    if cond is None:
                        cp.wait_recv()
                    else:
                        pl.when(cond)(cp.wait_recv)
        for h in range(2):
            k = h * C_IN + j
            for i in range(2):
                w_copy(i, k).wait()

            def tile(i, carry, k=k, first=(j == 0 and h == 0)):
                n = al((i % (ff // nt)) * nt, nt)
                m = al((i // (ff // nt)) * mt, mt)
                left = gat[k, pl.ds(m, mt), :]
                for w, acc in ((wg, acc_g), (wu, acc_u)):
                    v = jnp.dot(left, w[pl.ds(k * wi, wi), pl.ds(n, nt)], preferred_element_type=F32)
                    if first:
                        acc[pl.ds(m, mt), pl.ds(n, nt)] = v
                    else:
                        acc[pl.ds(m, mt), pl.ds(n, nt)] += v
                return carry
            lax.fori_loop(0, (ff // nt) * (total // mt), tile, 0)

    for n, xb, zb in chips():
        dx, dz = (n + 1) // nz, (n + 1) % nz
        p = gts.at[rows_of(lax.rem(x + nx - dx, nx), lax.rem(z + nz - dz, nz)), :]
        rc(p, p, gts_s.at[n], gts_r.at[n], grp=xb * 2 + c, loc=zb).wait_recv()

    def hidden_tile(i, carry):
        m = al(i * mt, mt)
        v = acc_g[pl.ds(m, mt), :]
        hid[pl.ds(m, mt), :] = (v / (1.0 + jnp.exp(-v)) * acc_u[pl.ds(m, mt), :]).astype(BF16)
        return carry
    lax.fori_loop(0, total // mt, hidden_tile, 0)

    expert = (g * nz + z) // (nz // EXP_GROUP)

    def down(h, j, m):
        y = jnp.dot(hid[pl.ds(m, mt), :], wd[h * C_OUT + j], preferred_element_type=F32)
        at = lax.broadcasted_iota(jnp.int32, (mt, LANES), 1)
        w = jnp.where(at == expert, gts[pl.ds(m, mt), :].astype(F32), 0.0)
        return y * jnp.sum(w, axis=1, keepdims=True)

    def core_out(j):
        return rc(snd.at[j], tin.at[j], ss.at[j], sr.at[j], grp=mate)

    span = nz * blk

    def x_out(j, xd, to):
        return rc(tin.at[j, pl.ds(al(to * span, span), span), :], xin.at[j, xd - 1],
                  xos.at[j, xd - 1], xor.at[j, xd - 1], grp=to * 2 + c)

    def down_other(j):
        wd_copy(other, j).wait()

        def tile(i, carry):
            m = al(i * mt, mt)
            snd[j, pl.ds(m, mt), :] = down(other, j, m).astype(BF16)
            return carry
        lax.fori_loop(0, total // mt, tile, 0)
        core_out(j).start()

    def down_own(j):
        wd_copy(c, j).wait()
        core_out(j).wait_recv()

        def tile(i, carry):
            m = al(i * mt, mt)
            tin[j, pl.ds(m, mt), :] = (down(c, j, m) + tin[j, pl.ds(m, mt), :].astype(F32)).astype(BF16)
            return carry
        lax.fori_loop(0, total // mt, tile, 0)
        for xd in range(1, nx):
            go(None, x_out(j, xd, lax.rem(x + xd, nx)))

    down_other(0)
    for j in range(C_OUT):
        if j + 1 < C_OUT:
            down_other(j + 1)
        down_own(j)

    def z_out(way, j, t):
        src, dst = ((zsr, zl), (zsl, zr))[way]
        return rc(src.at[j, t - 1], dst.at[j, t - 1], zos.at[way, j, t - 1], zor.at[way, j, t - 1],
                  loc=z + 1 if way == 0 else z - 1)

    for j in range(C_OUT):
        for xd in range(1, nx):
            x_out(j, xd, x).wait_recv()

        def q(zb):
            v = tin[j, rows_of(x, zb), :].astype(F32)
            for xd in range(1, nx):
                v = v + xin[j, xd - 1, pl.ds(al(zb * blk, blk), blk), :].astype(F32)
            return v

        for t in range(nz - 1, 0, -1):
            for way in range(2):
                buf, into = ((zsr, zl), (zsl, zr))[way]
                zb = z + t if way == 0 else z - t
                reach = z + t < nz if way == 0 else z >= t
                edge = z == 0 if way == 0 else z == nz - 1

                @pl.when(jnp.logical_and(reach, edge))
                def _():
                    buf[j, t - 1] = q(zb).astype(BF16)
                if t < nz - 1:
                    @pl.when(jnp.logical_and(reach, jnp.logical_not(edge)))
                    def _():
                        z_out(way, j, t + 1).wait_recv()
                        buf[j, t - 1] = (q(zb) + into[j, t].astype(F32)).astype(BF16)
                go(reach, z_out(way, j, t))
        res[...] = q(z)
        for way in range(2):
            into = (zl, zr)[way]

            @pl.when(can[1 - way])
            def _():
                z_out(way, j, 1).wait_recv()
                res[...] += into[j, 0].astype(F32)
        v = res[...]
        fin[j] = v.astype(BF16)
        go(None, rc(fin.at[j], fin_in.at[j], fs.at[j], fr.at[j], grp=mate))
        out_ref[:, pl.ds(al(c * half + j * wo, LANES), wo)] = jnp.where(c == 0, v[:rows], v[rows:]).astype(BF16)

    for j in range(C_OUT):
        rc(fin.at[j], fin_in.at[j], fs.at[j], fr.at[j], grp=mate).wait_recv()
        v = fin_in[j].astype(F32)
        out_ref[:, pl.ds(al(other * half + j * wo, LANES), wo)] = jnp.where(c == 0, v[:rows], v[rows:]).astype(BF16)

    swap.wait_send()
    for j in range(C_OUT):
        core_out(j).wait_send()
    for cond, cp in sends:
        if cond is None:
            cp.wait_send()
        else:
            pl.when(cond)(cp.wait_send)


def body(tokens, expert_ids, gate_values, w_gate, w_up, w_down):
    rows, width = tokens.shape
    nx = lax.axis_size("grp") // 2
    nz = lax.axis_size("loc")
    half = width // 2
    blk = 2 * rows
    total = nx * nz * blk
    ff = w_gate.shape[2]
    wi, wo = half // C_IN, half // C_OUT
    dma = pltpu.SemaphoreType.DMA
    ns = 2 * nz - 1
    vm = pltpu.VMEM
    scratch = [
        vm((width, ff), BF16), vm((width, ff), BF16), vm((2 * C_OUT, ff, wo), BF16),
        vm((blk, half + LANES), BF16), vm((blk, half + LANES), BF16),
        vm((2 * C_IN, total, wi), BF16), vm((total, LANES), BF16),
        vm((total, ff), F32), vm((total, ff), F32), vm((total, ff), BF16),
        vm((C_OUT, total, wo), BF16), vm((C_OUT, total, wo), BF16),
        vm((C_OUT, nx - 1, nz * blk, wo), BF16),
        vm((C_OUT, nz - 1, blk, wo), BF16), vm((C_OUT, nz - 1, blk, wo), BF16),
        vm((C_OUT, nz - 1, blk, wo), BF16), vm((C_OUT, nz - 1, blk, wo), BF16),
        vm((blk, wo), F32), vm((C_OUT, blk, wo), BF16), vm((C_OUT, blk, wo), BF16),
        dma((2, 2 * C_IN)), dma((2 * C_OUT,)), dma((2,)), dma((nx * nz - 1,)), dma((nx * nz - 1,)),
        dma((2, C_IN, nz - 1)), dma((2, C_IN, nz - 1)),
        dma((C_IN, nx - 1, ns)), dma((C_IN, nx - 1, ns)),
        dma((C_IN, nx, ns)), dma((C_IN, nx, ns)),
        dma((C_OUT,)), dma((C_OUT,)), dma((C_OUT, nx - 1)), dma((C_OUT, nx - 1)),
        dma((2, C_OUT, nz - 1)), dma((2, C_OUT, nz - 1)), dma((C_OUT,)), dma((C_OUT,)),
    ]
    inside = pl.BlockSpec(memory_space=pltpu.VMEM)
    outside = pl.BlockSpec(memory_space=pl.ANY)
    return pl.pallas_call(
        functools.partial(kernel, nx, nz),
        out_shape=jax.ShapeDtypeStruct((rows, width), BF16),
        in_specs=[inside] * 3 + [outside] * 3,
        out_specs=inside,
        scratch_shapes=scratch,
        compiler_params=pltpu.CompilerParams(
            collective_id=0, has_side_effects=True, vmem_limit_bytes=63 * 1024 * 1024),
    )(tokens, expert_ids, gate_values, w_gate, w_up, w_down)


def solution(mesh):
    placed = (
        P(("rep", "grp", "loc"), None),
        P(("rep", "grp", "loc"), None),
        P(("rep", "grp", "loc"), None),
        P(("grp", "loc"), None, None),
        P(("grp", "loc"), None, None),
        P(("grp", "loc"), None, None),
    )
    return jax.shard_map(
        body, mesh=mesh, in_specs=placed, out_specs=P(("rep", "grp", "loc"), None), check_vma=False
    )
```

```python
import functools

import jax
import jax.numpy as jnp
from jax import lax
from jax.experimental import pallas as pl
from jax.experimental.pallas import tpu as pltpu
from jax.sharding import PartitionSpec as P

EXP_GROUP = 4
LANES = 128
C_IN = 2
C_OUT = 4
F32 = jnp.float32
BF16 = jnp.bfloat16


def al(v, m):
    return pl.multiple_of(v, m)


def kernel(nx, nz, tok_ref, ids_ref, gv_ref, wg_hbm, wu_hbm, wd_hbm, out_ref,
           wg, wu, wd, pk, pk_in, gat, gts, acc_g, acc_u, hid, snd, tin, xin, zout, zin, res, fin, fin_in,
           w_sem, wd_sem, pk_sem, gts_s, gts_r, zs, zv, xs, xv, cs, cv, ss, sr, xos, xor, zos, zor, fs, fr):
    rows, width = tok_ref.shape
    half = width // 2
    blk = 2 * rows
    nb = nx * nz
    total = nb * blk
    wi = half // C_IN
    wo = half // C_OUT
    ff = wg.shape[1]
    g = lax.axis_index("grp")
    z = lax.axis_index("loc")
    x = g // 2
    c = g % 2
    other = 1 - c
    mate = x * 2 + other

    def rc(src, dst, s, r, grp=None, loc=None):
        return pltpu.make_async_remote_copy(
            src_ref=src, dst_ref=dst, send_sem=s, recv_sem=r,
            device_id={"grp": g if grp is None else grp, "loc": z if loc is None else loc},
            device_id_type=pl.DeviceIdType.MESH)

    def w_copy(i, k):
        src, dst = ((wg_hbm, wg), (wu_hbm, wu))[i]
        return pltpu.make_async_copy(src.at[0, pl.ds(k * wi, wi), :], dst.at[pl.ds(k * wi, wi), :], w_sem.at[i, k])

    def wd_copy(h, j):
        return pltpu.make_async_copy(
            wd_hbm.at[0, :, pl.ds(al(h * half + j * wo, LANES), wo)], wd.at[h * C_OUT + j], wd_sem.at[h * C_OUT + j])

    for j in range(C_IN):
        for h in range(2):
            for i in range(2):
                w_copy(i, h * C_IN + j).start()
    for j in range(C_OUT):
        wd_copy(other, j).start()
        wd_copy(c, j).start()

    barrier = pltpu.get_barrier_semaphore()

    def chips():
        for dx in range(nx):
            for dz in range(nz):
                if dx or dz:
                    yield dx * nz + dz - 1, lax.rem(x + dx, nx), lax.rem(z + dz, nz)

    pl.semaphore_signal(barrier, inc=1, device_id={"grp": mate, "loc": z}, device_id_type=pl.DeviceIdType.MESH)
    for _, xb, zb in chips():
        pl.semaphore_signal(barrier, inc=1, device_id={"grp": xb * 2 + c, "loc": zb},
                            device_id_type=pl.DeviceIdType.MESH)

    tok = tok_ref[...].astype(F32)
    lane = lax.broadcasted_iota(jnp.int32, (rows, LANES), 1)
    ids = ids_ref[...]
    gv = gv_ref[...].astype(F32)
    dense = jnp.zeros((rows, LANES), F32)
    for k in range(ids.shape[1]):
        dense = dense + jnp.where(lane == ids[:, k:k + 1], gv[:, k:k + 1], 0.0)
    pk[:, :half] = jnp.concatenate([tok[:, :half], tok[:, half:]], axis=0).astype(BF16)
    pk[:, half:] = jnp.concatenate([dense, dense], axis=0).astype(BF16)
    pl.semaphore_wait(barrier, nb)
    swap = rc(pk, pk_in, pk_sem.at[0], pk_sem.at[1], grp=mate)
    swap.start()

    def rows_of(xb, zb):
        return pl.ds(al((xb * nz + zb) * blk, blk), blk)

    swap.wait_recv()
    mine, theirs = pk[...].astype(F32), pk_in[...].astype(F32)
    a = jnp.where(c == 0, mine, theirs)
    b = jnp.where(c == 0, theirs, mine)
    for h in range(2):
        both = jnp.concatenate([a[h * rows:(h + 1) * rows, :half], b[h * rows:(h + 1) * rows, :half]], axis=0)
        both = both.astype(BF16)
        for j in range(C_IN):
            gat[h * C_IN + j, rows_of(x, z), :] = both[:, j * wi:(j + 1) * wi]
    gts[rows_of(x, z), :] = jnp.concatenate([a[:rows, half:], b[:rows, half:]], axis=0).astype(BF16)

    sends = []

    def go(cond, cp):
        sends.append((cond, cp))
        if cond is None:
            cp.start()
        else:
            pl.when(cond)(cp.start)

    def piece(h, j, xb, zb):
        return gat.at[h * C_IN + j, rows_of(xb, zb), :]

    def zcopy(way, j, d, zb, to):
        p = piece(c, j, x, zb)
        return rc(p, p, zs.at[way, j, d - 1], zv.at[way, j, d - 1], loc=to)

    def xcopy(j, xd, slot, xb, zb, to):
        p = piece(c, j, xb, zb)
        return rc(p, p, xs.at[j, xd - 1, slot], xv.at[j, xd - 1, slot], grp=to * 2 + c)

    def ccopy(h, j, xd, slot, xb, zb):
        p = piece(h, j, xb, zb)
        return rc(p, p, cs.at[j, xd, slot], cv.at[j, xd, slot], grp=mate)

    def reach(way, d):
        return z + d < nz if way == 0 else z >= d

    def spread(cond, j, slot, zb):
        for xd in range(1, nx):
            go(cond, xcopy(j, xd, slot, x, zb, lax.rem(x + xd, nx)))

    for d in range(1, nz):
        for j in range(C_IN):
            for way in range(2):
                go(reach(way, d), zcopy(way, j, d, z, z + d if way == 0 else z - d))
            if d == 1:
                spread(None, j, 0, z)
    for n, xb, zb in chips():
        p = gts.at[rows_of(x, z), :]
        go(None, rc(p, p, gts_s.at[n], gts_r.at[n], grp=xb * 2 + c, loc=zb))

    def slots(d):
        if d == 0:
            return [(None, 0, z)]
        return [(z >= d, d, z - d), (z + d < nz, nz - 1 + d, z + d)]

    def x_arrivals(d, j):
        for cond, slot, zb in slots(d):
            for xd in range(1, nx):
                xb = lax.rem(x + nx - xd, nx)

                def take():
                    xcopy(j, xd, slot, xb, zb, x).wait_recv()
                    ccopy(c, j, xd, slot, xb, zb).start()
                if cond is None:
                    take()
                else:
                    pl.when(cond)(take)
                sends.append((cond, ccopy(c, j, xd, slot, xb, zb)))

    for d in range(1, nz):
        for j in range(C_IN):
            for way, (cond, slot, zb) in enumerate(slots(d)):
                pl.when(cond)(zcopy(way, j, d, zb, z).wait_recv)
                spread(cond, j, slot, zb)
                go(cond, ccopy(c, j, 0, slot, x, zb))
            x_arrivals(d - 1, j)
    for j in range(C_IN):
        x_arrivals(nz - 1, j)

    mt = min(LANES, total)
    nt = min(256, ff)
    for j in range(C_IN):
        for d in range(nz):
            for cond, slot, zb in slots(d):
                for xd in range(0 if d else 1, nx):
                    cp = ccopy(other, j, xd, slot, lax.rem(x + nx - xd, nx), zb)
                    if cond is None:
                        cp.wait_recv()
                    else:
                        pl.when(cond)(cp.wait_recv)
        for h in range(2):
            k = h * C_IN + j
            for i in range(2):
                w_copy(i, k).wait()

            def tile(i, carry, k=k, first=(j == 0 and h == 0)):
                n = al((i % (ff // nt)) * nt, nt)
                m = al((i // (ff // nt)) * mt, mt)
                left = gat[k, pl.ds(m, mt), :]
                for w, acc in ((wg, acc_g), (wu, acc_u)):
                    v = jnp.dot(left, w[pl.ds(k * wi, wi), pl.ds(n, nt)], preferred_element_type=F32)
                    if first:
                        acc[pl.ds(m, mt), pl.ds(n, nt)] = v
                    else:
                        acc[pl.ds(m, mt), pl.ds(n, nt)] += v
                return carry
            lax.fori_loop(0, (ff // nt) * (total // mt), tile, 0)

    for n, xb, zb in chips():
        dx, dz = (n + 1) // nz, (n + 1) % nz
        p = gts.at[rows_of(lax.rem(x + nx - dx, nx), lax.rem(z + nz - dz, nz)), :]
        rc(p, p, gts_s.at[n], gts_r.at[n], grp=xb * 2 + c, loc=zb).wait_recv()

    def hidden_tile(i, carry):
        m = al(i * mt, mt)
        v = acc_g[pl.ds(m, mt), :]
        hid[pl.ds(m, mt), :] = (v / (1.0 + jnp.exp(-v)) * acc_u[pl.ds(m, mt), :]).astype(BF16)
        return carry
    lax.fori_loop(0, total // mt, hidden_tile, 0)

    expert = (g * nz + z) // (nz // EXP_GROUP)

    def down(h, j, m):
        y = jnp.dot(hid[pl.ds(m, mt), :], wd[h * C_OUT + j], preferred_element_type=F32)
        at = lax.broadcasted_iota(jnp.int32, (mt, LANES), 1)
        w = jnp.where(at == expert, gts[pl.ds(m, mt), :].astype(F32), 0.0)
        return y * jnp.sum(w, axis=1, keepdims=True)

    def core_out(j):
        return rc(snd.at[j], tin.at[j], ss.at[j], sr.at[j], grp=mate)

    span = nz * blk

    def x_out(j, xd, to):
        return rc(tin.at[j, pl.ds(al(to * span, span), span), :], xin.at[j, xd - 1],
                  xos.at[j, xd - 1], xor.at[j, xd - 1], grp=to * 2 + c)

    def down_other(j):
        wd_copy(other, j).wait()

        def tile(i, carry):
            m = al(i * mt, mt)
            snd[j, pl.ds(m, mt), :] = down(other, j, m).astype(BF16)
            return carry
        lax.fori_loop(0, total // mt, tile, 0)
        core_out(j).start()

    def down_own(j):
        wd_copy(c, j).wait()
        core_out(j).wait_recv()

        def tile(i, carry):
            m = al(i * mt, mt)
            tin[j, pl.ds(m, mt), :] = (down(c, j, m) + tin[j, pl.ds(m, mt), :].astype(F32)).astype(BF16)
            return carry
        lax.fori_loop(0, total // mt, tile, 0)
        for xd in range(1, nx):
            go(None, x_out(j, xd, lax.rem(x + xd, nx)))

    down_other(0)
    for j in range(C_OUT):
        if j + 1 < C_OUT:
            down_other(j + 1)
        down_own(j)

    def z_out(way, j, d, to):
        return rc(zout.at[j, to], zin.at[way, j, d - 1], zos.at[way, j, d - 1], zor.at[way, j, d - 1], loc=to)

    def sum_x(j):
        for xd in range(1, nx):
            x_out(j, xd, x).wait_recv()

        def q(zb):
            v = tin[j, rows_of(x, zb), :].astype(F32)
            for xd in range(1, nx):
                v = v + xin[j, xd - 1, pl.ds(al(zb * blk, blk), blk), :].astype(F32)
            return v

        for d in range(nz - 1, 0, -1):
            for way in range(2):
                zb = z + d if way == 0 else z - d

                @pl.when(reach(way, d))
                def _():
                    zout[j, zb] = q(zb).astype(BF16)
                go(reach(way, d), z_out(way, j, d, zb))
        res[j] = q(z)

    def sum_z(j):
        for d in range(1, nz):
            for way in range(2):
                @pl.when(reach(1 - way, d))
                def _():
                    z_out(way, j, d, z).wait_recv()
                    res[j] += zin[way, j, d - 1].astype(F32)
        v = res[j]
        fin[j] = v.astype(BF16)
        go(None, rc(fin.at[j], fin_in.at[j], fs.at[j], fr.at[j], grp=mate))
        out_ref[:, pl.ds(al(c * half + j * wo, LANES), wo)] = jnp.where(c == 0, v[:rows], v[rows:]).astype(BF16)

    for j in range(C_OUT):
        sum_x(j)
        if j:
            sum_z(j - 1)
    sum_z(C_OUT - 1)

    for j in range(C_OUT):
        rc(fin.at[j], fin_in.at[j], fs.at[j], fr.at[j], grp=mate).wait_recv()
        v = fin_in[j].astype(F32)
        out_ref[:, pl.ds(al(other * half + j * wo, LANES), wo)] = jnp.where(c == 0, v[:rows], v[rows:]).astype(BF16)

    swap.wait_send()
    for j in range(C_OUT):
        core_out(j).wait_send()
    for cond, cp in sends:
        if cond is None:
            cp.wait_send()
        else:
            pl.when(cond)(cp.wait_send)


def body(tokens, expert_ids, gate_values, w_gate, w_up, w_down):
    rows, width = tokens.shape
    nx = lax.axis_size("grp") // 2
    nz = lax.axis_size("loc")
    half = width // 2
    blk = 2 * rows
    total = nx * nz * blk
    ff = w_gate.shape[2]
    wi, wo = half // C_IN, half // C_OUT
    dma = pltpu.SemaphoreType.DMA
    ns = 2 * nz - 1
    vm = pltpu.VMEM
    scratch = [
        vm((width, ff), BF16), vm((width, ff), BF16), vm((2 * C_OUT, ff, wo), BF16),
        vm((blk, half + LANES), BF16), vm((blk, half + LANES), BF16),
        vm((2 * C_IN, total, wi), BF16), vm((total, LANES), BF16),
        vm((total, ff), F32), vm((total, ff), F32), vm((total, ff), BF16),
        vm((C_OUT, total, wo), BF16), vm((C_OUT, total, wo), BF16),
        vm((C_OUT, nx - 1, nz * blk, wo), BF16),
        vm((C_OUT, nz, blk, wo), BF16), vm((2, C_OUT, nz - 1, blk, wo), BF16),
        vm((C_OUT, blk, wo), F32), vm((C_OUT, blk, wo), BF16), vm((C_OUT, blk, wo), BF16),
        dma((2, 2 * C_IN)), dma((2 * C_OUT,)), dma((2,)), dma((nx * nz - 1,)), dma((nx * nz - 1,)),
        dma((2, C_IN, nz - 1)), dma((2, C_IN, nz - 1)),
        dma((C_IN, nx - 1, ns)), dma((C_IN, nx - 1, ns)),
        dma((C_IN, nx, ns)), dma((C_IN, nx, ns)),
        dma((C_OUT,)), dma((C_OUT,)), dma((C_OUT, nx - 1)), dma((C_OUT, nx - 1)),
        dma((2, C_OUT, nz - 1)), dma((2, C_OUT, nz - 1)), dma((C_OUT,)), dma((C_OUT,)),
    ]
    inside = pl.BlockSpec(memory_space=pltpu.VMEM)
    outside = pl.BlockSpec(memory_space=pl.ANY)
    return pl.pallas_call(
        functools.partial(kernel, nx, nz),
        out_shape=jax.ShapeDtypeStruct((rows, width), BF16),
        in_specs=[inside] * 3 + [outside] * 3,
        out_specs=inside,
        scratch_shapes=scratch,
        compiler_params=pltpu.CompilerParams(
            collective_id=0, has_side_effects=True, vmem_limit_bytes=63 * 1024 * 1024),
    )(tokens, expert_ids, gate_values, w_gate, w_up, w_down)


def solution(mesh):
    placed = (
        P(("rep", "grp", "loc"), None),
        P(("rep", "grp", "loc"), None),
        P(("rep", "grp", "loc"), None),
        P(("grp", "loc"), None, None),
        P(("grp", "loc"), None, None),
        P(("grp", "loc"), None, None),
    )
    return jax.shard_map(
        body, mesh=mesh, in_specs=placed, out_specs=P(("rep", "grp", "loc"), None), check_vma=False
    )
```

```python
import functools

import jax
import jax.numpy as jnp
from jax import lax
from jax.experimental import pallas as pl
from jax.experimental.pallas import tpu as pltpu
from jax.sharding import PartitionSpec as P

EXP_GROUP = 4
LANES = 128
C_IN = 2
C_OUT = 4
F32 = jnp.float32
BF16 = jnp.bfloat16


def al(v, m):
    return pl.multiple_of(v, m)


def kernel(nx, nz, tok_ref, ids_ref, gv_ref, wg_hbm, wu_hbm, wd_hbm, out_ref,
           wg, wu, wd, pk, pk_in, gat, gts, acc_g, acc_u, hid, snd, tin, xin, zout, zin, res, fin, fin_in,
           w_sem, wd_sem, pk_sem, gts_s, gts_r, zs, zv, xs, xv, cs, cv, ss, sr, xos, xor, zos, zor, fs, fr):
    rows, width = tok_ref.shape
    half = width // 2
    blk = 2 * rows
    nb = nx * nz
    total = nb * blk
    wi = half // C_IN
    wo = half // C_OUT
    ff = wg.shape[1]
    g = lax.axis_index("grp")
    z = lax.axis_index("loc")
    x = g // 2
    c = g % 2
    other = 1 - c
    mate = x * 2 + other

    def rc(src, dst, s, r, grp=None, loc=None):
        return pltpu.make_async_remote_copy(
            src_ref=src, dst_ref=dst, send_sem=s, recv_sem=r,
            device_id={"grp": g if grp is None else grp, "loc": z if loc is None else loc},
            device_id_type=pl.DeviceIdType.MESH)

    def w_copy(i, k):
        src, dst = ((wg_hbm, wg), (wu_hbm, wu))[i]
        return pltpu.make_async_copy(src.at[0, pl.ds(k * wi, wi), :], dst.at[pl.ds(k * wi, wi), :], w_sem.at[i, k])

    def wd_copy(h, j):
        return pltpu.make_async_copy(
            wd_hbm.at[0, :, pl.ds(al(h * half + j * wo, LANES), wo)], wd.at[h * C_OUT + j], wd_sem.at[h * C_OUT + j])

    for j in range(C_IN):
        for h in range(2):
            for i in range(2):
                w_copy(i, h * C_IN + j).start()
    for j in range(C_OUT):
        wd_copy(other, j).start()
        wd_copy(c, j).start()

    barrier = pltpu.get_barrier_semaphore()

    def chips():
        for dx in range(nx):
            for dz in range(nz):
                if dx or dz:
                    yield dx * nz + dz - 1, lax.rem(x + dx, nx), lax.rem(z + dz, nz)

    pl.semaphore_signal(barrier, inc=1, device_id={"grp": mate, "loc": z}, device_id_type=pl.DeviceIdType.MESH)
    for _, xb, zb in chips():
        pl.semaphore_signal(barrier, inc=1, device_id={"grp": xb * 2 + c, "loc": zb},
                            device_id_type=pl.DeviceIdType.MESH)

    tok = tok_ref[...].astype(F32)
    lane = lax.broadcasted_iota(jnp.int32, (rows, LANES), 1)
    ids = ids_ref[...]
    gv = gv_ref[...].astype(F32)
    dense = jnp.zeros((rows, LANES), F32)
    for k in range(ids.shape[1]):
        dense = dense + jnp.where(lane == ids[:, k:k + 1], gv[:, k:k + 1], 0.0)
    pk[:, :half] = jnp.concatenate([tok[:, :half], tok[:, half:]], axis=0).astype(BF16)
    pk[:, half:] = jnp.concatenate([dense, dense], axis=0).astype(BF16)
    pl.semaphore_wait(barrier, nb)
    swap = rc(pk, pk_in, pk_sem.at[0], pk_sem.at[1], grp=mate)
    swap.start()

    def rows_of(xb, zb):
        return pl.ds(al((xb * nz + zb) * blk, blk), blk)

    swap.wait_recv()
    mine, theirs = pk[...].astype(F32), pk_in[...].astype(F32)
    a = jnp.where(c == 0, mine, theirs)
    b = jnp.where(c == 0, theirs, mine)
    for h in range(2):
        both = jnp.concatenate([a[h * rows:(h + 1) * rows, :half], b[h * rows:(h + 1) * rows, :half]], axis=0)
        both = both.astype(BF16)
        for j in range(C_IN):
            gat[h * C_IN + j, rows_of(x, z), :] = both[:, j * wi:(j + 1) * wi]
    gts[rows_of(x, z), :] = jnp.concatenate([a[:rows, half:], b[:rows, half:]], axis=0).astype(BF16)

    sends = []

    def go(cond, cp):
        sends.append((cond, cp))
        if cond is None:
            cp.start()
        else:
            pl.when(cond)(cp.start)

    def both_conds(p, q):
        return p if q is None else q if p is None else jnp.logical_and(p, q)

    def piece(h, j, xb, zb):
        return gat.at[h * C_IN + j, rows_of(xb, zb), :]

    def zcopy(way, j, d, zb):
        p = piece(c, j, x, zb)
        return rc(p, p, zs.at[way, j, d], zv.at[way, j, d], loc=z + 1 if way == 0 else z - 1)

    def xcopy(j, xd, slot, xb, zb, to):
        p = piece(c, j, xb, zb)
        return rc(p, p, xs.at[j, xd - 1, slot], xv.at[j, xd - 1, slot], grp=to * 2 + c)

    def ccopy(h, j, xd, slot, xb, zb):
        p = piece(h, j, xb, zb)
        return rc(p, p, cs.at[j, xd, slot], cv.at[j, xd, slot], grp=mate)

    can = (z + 1 < nz, z >= 1)

    def spread(cond, j, slot, zb):
        for xd in range(1, nx):
            go(cond, xcopy(j, xd, slot, x, zb, lax.rem(x + xd, nx)))

    for j in range(C_IN):
        for way in range(2):
            go(can[way], zcopy(way, j, 0, z))
        spread(None, j, 0, z)
    for n, xb, zb in chips():
        p = gts.at[rows_of(x, z), :]
        go(None, rc(p, p, gts_s.at[n], gts_r.at[n], grp=xb * 2 + c, loc=zb))

    def slots(d):
        if d == 0:
            return [(None, 0, z)]
        return [(z >= d, d, z - d), (z + d < nz, nz - 1 + d, z + d)]

    def x_arrivals(d, j):
        for cond, slot, zb in slots(d):
            for xd in range(1, nx):
                xb = lax.rem(x + nx - xd, nx)

                def take():
                    xcopy(j, xd, slot, xb, zb, x).wait_recv()
                    ccopy(c, j, xd, slot, xb, zb).start()
                if cond is None:
                    take()
                else:
                    pl.when(cond)(take)
                sends.append((cond, ccopy(c, j, xd, slot, xb, zb)))

    for d in range(1, nz):
        for j in range(C_IN):
            for way, (cond, slot, zb) in enumerate(slots(d)):
                pl.when(cond)(zcopy(way, j, d - 1, zb).wait_recv)
                if d < nz - 1:
                    go(both_conds(cond, can[way]), zcopy(way, j, d, zb))
                spread(cond, j, slot, zb)
                go(cond, ccopy(c, j, 0, slot, x, zb))
            x_arrivals(d - 1, j)
    for j in range(C_IN):
        x_arrivals(nz - 1, j)

    mt = min(LANES, total)
    nt = min(256, ff)
    for j in range(C_IN):
        for d in range(nz):
            for cond, slot, zb in slots(d):
                for xd in range(0 if d else 1, nx):
                    cp = ccopy(other, j, xd, slot, lax.rem(x + nx - xd, nx), zb)
                    if cond is None:
                        cp.wait_recv()
                    else:
                        pl.when(cond)(cp.wait_recv)
        for h in range(2):
            k = h * C_IN + j
            for i in range(2):
                w_copy(i, k).wait()

            def tile(i, carry, k=k, first=(j == 0 and h == 0)):
                n = al((i % (ff // nt)) * nt, nt)
                m = al((i // (ff // nt)) * mt, mt)
                left = gat[k, pl.ds(m, mt), :]
                for w, acc in ((wg, acc_g), (wu, acc_u)):
                    v = jnp.dot(left, w[pl.ds(k * wi, wi), pl.ds(n, nt)], preferred_element_type=F32)
                    if first:
                        acc[pl.ds(m, mt), pl.ds(n, nt)] = v
                    else:
                        acc[pl.ds(m, mt), pl.ds(n, nt)] += v
                return carry
            lax.fori_loop(0, (ff // nt) * (total // mt), tile, 0)

    for n, xb, zb in chips():
        dx, dz = (n + 1) // nz, (n + 1) % nz
        p = gts.at[rows_of(lax.rem(x + nx - dx, nx), lax.rem(z + nz - dz, nz)), :]
        rc(p, p, gts_s.at[n], gts_r.at[n], grp=xb * 2 + c, loc=zb).wait_recv()

    def hidden_tile(i, carry):
        m = al(i * mt, mt)
        v = acc_g[pl.ds(m, mt), :]
        hid[pl.ds(m, mt), :] = (v / (1.0 + jnp.exp(-v)) * acc_u[pl.ds(m, mt), :]).astype(BF16)
        return carry
    lax.fori_loop(0, total // mt, hidden_tile, 0)

    expert = (g * nz + z) // (nz // EXP_GROUP)

    def down(h, j, m):
        y = jnp.dot(hid[pl.ds(m, mt), :], wd[h * C_OUT + j], preferred_element_type=F32)
        at = lax.broadcasted_iota(jnp.int32, (mt, LANES), 1)
        w = jnp.where(at == expert, gts[pl.ds(m, mt), :].astype(F32), 0.0)
        return y * jnp.sum(w, axis=1, keepdims=True)

    def core_out(j):
        return rc(snd.at[j], tin.at[j], ss.at[j], sr.at[j], grp=mate)

    span = nz * blk

    def x_out(j, xd, to):
        return rc(tin.at[j, pl.ds(al(to * span, span), span), :], xin.at[j, xd - 1],
                  xos.at[j, xd - 1], xor.at[j, xd - 1], grp=to * 2 + c)

    def down_other(j):
        wd_copy(other, j).wait()

        def tile(i, carry):
            m = al(i * mt, mt)
            snd[j, pl.ds(m, mt), :] = down(other, j, m).astype(BF16)
            return carry
        lax.fori_loop(0, total // mt, tile, 0)
        core_out(j).start()

    def down_own(j):
        wd_copy(c, j).wait()
        core_out(j).wait_recv()

        def tile(i, carry):
            m = al(i * mt, mt)
            tin[j, pl.ds(m, mt), :] = (down(c, j, m) + tin[j, pl.ds(m, mt), :].astype(F32)).astype(BF16)
            return carry
        lax.fori_loop(0, total // mt, tile, 0)
        for xd in range(1, nx):
            go(None, x_out(j, xd, lax.rem(x + xd, nx)))

    down_other(0)
    for j in range(C_OUT):
        if j + 1 < C_OUT:
            down_other(j + 1)
        down_own(j)

    def z_out(way, j, d, to):
        return rc(zout.at[j, to], zin.at[way, j, d - 1], zos.at[way, j, d - 1], zor.at[way, j, d - 1], loc=to)

    def reach(way, d):
        return z + d < nz if way == 0 else z >= d

    def sum_x(j):
        for xd in range(1, nx):
            x_out(j, xd, x).wait_recv()

        def q(zb):
            v = tin[j, rows_of(x, zb), :].astype(F32)
            for xd in range(1, nx):
                v = v + xin[j, xd - 1, pl.ds(al(zb * blk, blk), blk), :].astype(F32)
            return v

        for d in range(nz - 1, 0, -1):
            for way in range(2):
                zb = z + d if way == 0 else z - d

                @pl.when(reach(way, d))
                def _():
                    zout[j, zb] = q(zb).astype(BF16)
                go(reach(way, d), z_out(way, j, d, zb))
        res[j] = q(z)

    def sum_z(j):
        for d in range(1, nz):
            for way in range(2):
                @pl.when(reach(1 - way, d))
                def _():
                    z_out(way, j, d, z).wait_recv()
                    res[j] += zin[way, j, d - 1].astype(F32)
        v = res[j]
        fin[j] = v.astype(BF16)
        go(None, rc(fin.at[j], fin_in.at[j], fs.at[j], fr.at[j], grp=mate))
        out_ref[:, pl.ds(al(c * half + j * wo, LANES), wo)] = jnp.where(c == 0, v[:rows], v[rows:]).astype(BF16)

    for j in range(C_OUT):
        sum_x(j)
        if j:
            sum_z(j - 1)
    sum_z(C_OUT - 1)

    for j in range(C_OUT):
        rc(fin.at[j], fin_in.at[j], fs.at[j], fr.at[j], grp=mate).wait_recv()
        v = fin_in[j].astype(F32)
        out_ref[:, pl.ds(al(other * half + j * wo, LANES), wo)] = jnp.where(c == 0, v[:rows], v[rows:]).astype(BF16)

    swap.wait_send()
    for j in range(C_OUT):
        core_out(j).wait_send()
    for cond, cp in sends:
        if cond is None:
            cp.wait_send()
        else:
            pl.when(cond)(cp.wait_send)


def body(tokens, expert_ids, gate_values, w_gate, w_up, w_down):
    rows, width = tokens.shape
    nx = lax.axis_size("grp") // 2
    nz = lax.axis_size("loc")
    half = width // 2
    blk = 2 * rows
    total = nx * nz * blk
    ff = w_gate.shape[2]
    wi, wo = half // C_IN, half // C_OUT
    dma = pltpu.SemaphoreType.DMA
    ns = 2 * nz - 1
    vm = pltpu.VMEM
    scratch = [
        vm((width, ff), BF16), vm((width, ff), BF16), vm((2 * C_OUT, ff, wo), BF16),
        vm((blk, half + LANES), BF16), vm((blk, half + LANES), BF16),
        vm((2 * C_IN, total, wi), BF16), vm((total, LANES), BF16),
        vm((total, ff), F32), vm((total, ff), F32), vm((total, ff), BF16),
        vm((C_OUT, total, wo), BF16), vm((C_OUT, total, wo), BF16),
        vm((C_OUT, nx - 1, nz * blk, wo), BF16),
        vm((C_OUT, nz, blk, wo), BF16), vm((2, C_OUT, nz - 1, blk, wo), BF16),
        vm((C_OUT, blk, wo), F32), vm((C_OUT, blk, wo), BF16), vm((C_OUT, blk, wo), BF16),
        dma((2, 2 * C_IN)), dma((2 * C_OUT,)), dma((2,)), dma((nx * nz - 1,)), dma((nx * nz - 1,)),
        dma((2, C_IN, nz - 1)), dma((2, C_IN, nz - 1)),
        dma((C_IN, nx - 1, ns)), dma((C_IN, nx - 1, ns)),
        dma((C_IN, nx, ns)), dma((C_IN, nx, ns)),
        dma((C_OUT,)), dma((C_OUT,)), dma((C_OUT, nx - 1)), dma((C_OUT, nx - 1)),
        dma((2, C_OUT, nz - 1)), dma((2, C_OUT, nz - 1)), dma((C_OUT,)), dma((C_OUT,)),
    ]
    inside = pl.BlockSpec(memory_space=pltpu.VMEM)
    outside = pl.BlockSpec(memory_space=pl.ANY)
    return pl.pallas_call(
        functools.partial(kernel, nx, nz),
        out_shape=jax.ShapeDtypeStruct((rows, width), BF16),
        in_specs=[inside] * 3 + [outside] * 3,
        out_specs=inside,
        scratch_shapes=scratch,
        compiler_params=pltpu.CompilerParams(
            collective_id=0, has_side_effects=True, vmem_limit_bytes=63 * 1024 * 1024),
    )(tokens, expert_ids, gate_values, w_gate, w_up, w_down)


def solution(mesh):
    placed = (
        P(("rep", "grp", "loc"), None),
        P(("rep", "grp", "loc"), None),
        P(("rep", "grp", "loc"), None),
        P(("grp", "loc"), None, None),
        P(("grp", "loc"), None, None),
        P(("grp", "loc"), None, None),
    )
    return jax.shard_map(
        body, mesh=mesh, in_specs=placed, out_specs=P(("rep", "grp", "loc"), None), check_vma=False
    )
```
